32 devices in a mesh: grp: 2 (over y), row: 4 (over z), col: 4 (over x, core).
Axes of the slice: x: 2, y: 2, z: 4, core: 2. Of those that a mesh axis runs over, the one named last changes fastest.
Arguments:
- src_elem: bfloat16 [4, 4, 512, 512], P('row', 'grp', 'col'), parts along dimension 1, may hold values from -0.25 to 0.25
- snk_elem: bfloat16 [8, 4, 512, 512], P('col', 'grp', 'row'), parts along dimension 1, may hold values from -0.25 to 0.25
- peramb: bfloat16 [4, 8, 4, 512, 512], P('row', 'col', 'grp'), parts along dimension 2, may hold values from -0.15625 to 0.15625
- insertions: int32 [2, 16], replicated, may hold values from 0 to 15, each once within a row
Outputs:
- blocks: float32 [2, 32, 4, 8], P(None, 'grp', 'row', 'col'), parts along dimension 1
The draws below stay inside these ranges and needn't reach their ends.
There are 2 independent parts, one for each index of `grp`. The reference program is written for one: setup_inputs(seed, part) draws one part's arguments, and reference() takes and returns one part's arrays. A program takes and returns all parts, laid end to end along the dimension named above; an argument that names none is the same for every part. Nothing has to cross between parts.
Inputs may be any that keep to these rules, and one draw needn't show every extreme that they name: Each of the two rows of insertions names every code once.
All inputs are finite; a program needn't handle non-finite values.
Results may differ from the reference program's by a relative error of at most 0.0003.
Values may be sent and summed in bfloat16 or wider, within the bound.
A program may use at most 64 MiB of HBM per device.

```python
import jax
import jax.numpy as jnp
import numpy as np
from jax import lax

NV = 128
DIM = 512
INSERTS = 16
TS = 4
TK = 8


def levels(rng, shape, split, smallest, high):
    gain, own = 1.0, jax.random.fold_in(rng, 6)
    for dim, blocks in split:
        draws = jnp.exp(jax.random.uniform(jax.random.fold_in(own, dim), (blocks,), jnp.float32, smallest / len(split), high / len(split)))
        gain = gain * jnp.repeat(draws, shape[dim] // blocks).reshape([-1 if axis == dim else 1 for axis in range(len(shape))])
    return gain


def normal_values(stream_key, dims, scale, reach, shards=(), kind=jnp.bfloat16):
    loudness = levels(stream_key, dims, shards, -0.22, 0.18) if shards else 1.0
    values = jax.random.normal(stream_key, dims, jnp.float32) * scale * loudness
    return jnp.minimum(jnp.maximum(values, -reach), reach).astype(kind)


def setup_inputs(seed: int = 0, part: int = 0) -> dict:
    key_list = jax.random.split(jax.random.key(seed), 5)
    own_keys = jax.random.split(jax.random.fold_in(key_list[4], part), 5)
    src_elem = normal_values(own_keys[0], (TS, 2, DIM, DIM), DIM ** -0.5, 0.25, ((0, 4), (2, 4)))
    snk_elem = normal_values(own_keys[1], (TK, 2, DIM, DIM), DIM ** -0.5, 0.25, ((0, 4), (2, 4)))
    peramb = normal_values(own_keys[2], (TS, TK, 2, DIM, DIM), (12 * NV) ** -0.5, 0.15625, ((0, 4), (1, 4)))
    insertions = jax.vmap(lambda own: jax.random.permutation(own, INSERTS))(jax.random.split(key_list[3], 2)).reshape((2, INSERTS)).astype(jnp.int32)
    return dict(src_elem=src_elem, snk_elem=snk_elem, peramb=peramb, insertions=insertions)


def gamma_tables():
    zeros_two = np.zeros((2, 2))
    pauli_re = [np.array([[0.0, 1.0], [1.0, 0.0]]), zeros_two, np.array([[1.0, 0.0], [0.0, -1.0]])]
    pauli_im = [zeros_two, np.array([[0.0, -1.0], [1.0, 0.0]]), zeros_two]
    basis_re = []
    basis_im = []
    for index in range(3):
        part_re = np.zeros((4, 4))
        part_im = np.zeros((4, 4))
        part_re[0:2, 2:4] = pauli_im[index]
        part_im[0:2, 2:4] = -pauli_re[index]
        part_re[2:4, 0:2] = -pauli_im[index]
        part_im[2:4, 0:2] = pauli_re[index]
        basis_re.append(part_re)
        basis_im.append(part_im)
    fourth_re = np.zeros((4, 4))
    fourth_re[0:2, 2:4] = np.eye(2)
    fourth_re[2:4, 0:2] = np.eye(2)
    basis_re.append(fourth_re)
    basis_im.append(np.zeros((4, 4)))
    tables_re = []
    tables_im = []
    for subset in range(16):
        prod_re = np.eye(4)
        prod_im = np.zeros((4, 4))
        for bit_index in range(4):
            if (subset >> bit_index) & 1:
                next_re = prod_re @ basis_re[bit_index] - prod_im @ basis_im[bit_index]
                next_im = prod_re @ basis_im[bit_index] + prod_im @ basis_re[bit_index]
                prod_re = next_re
                prod_im = next_im
        tables_re.append(prod_re)
        tables_im.append(prod_im)
    return np.stack(tables_re).astype(np.float32), np.stack(tables_im).astype(np.float32)


def sign_vector(order):
    spins = jnp.arange(order) // (order // 4)
    return jnp.where(spins < 2, 1.0, -1.0).astype(jnp.float32)


def dot_plain(left, right):
    return jnp.dot(left, right, preferred_element_type=jnp.float32)


def dot_trans(left, right):
    return lax.dot_general(left, right, (((1,), (1,)), ((), ())), preferred_element_type=jnp.float32)


def forward_rows(rows, pair):
    real_part = dot_plain(rows[0], pair[0]) - dot_plain(rows[1], pair[1])
    imag_part = dot_plain(rows[0], pair[1]) + dot_plain(rows[1], pair[0])
    return jnp.stack([real_part, imag_part])


def backward_rows(rows, pair, signs):
    signed = rows * signs.astype(rows.dtype)[None, None, :]
    real_part = dot_trans(signed[0], pair[0]) + dot_trans(signed[1], pair[1])
    imag_part = dot_trans(signed[1], pair[0]) - dot_trans(signed[0], pair[1])
    return jnp.stack([real_part, imag_part]) * signs[None, None, :]


def spin_block(forward, backward):
    order = forward.shape[-1]
    evecs = order // 4
    fwd = forward.reshape(2, 4, evecs, 4, evecs)
    bwd = backward.reshape(2, 4, evecs, 4, evecs)
    high = lax.Precision.HIGHEST

    def contract(left, right):
        return jnp.einsum("uavb,wbsa->uvws", left, right, precision=high)

    real_part = contract(fwd[0], bwd[0]) - contract(fwd[1], bwd[1])
    imag_part = contract(fwd[0], bwd[1]) + contract(fwd[1], bwd[0])
    return jnp.stack([real_part, imag_part])


def insert_gammas(spin_all, insertions):
    table_re, table_im = gamma_tables()
    high = lax.Precision.HIGHEST
    codes = jnp.arange(16)

    def select(which):
        onehot = (insertions[which][:, None] == codes[None, :]).astype(jnp.float32)
        sel_re = jnp.dot(onehot, jnp.asarray(table_re).reshape(16, 16), precision=high).reshape(-1, 4, 4)
        sel_im = jnp.dot(onehot, jnp.asarray(table_im).reshape(16, 16), precision=high).reshape(-1, 4, 4)
        return sel_re, sel_im

    first_re, first_im = select(0)
    second_re, second_im = select(1)
    outer_re = jnp.einsum("ksu,kvw->ksuvw", first_re, second_re, precision=high) - jnp.einsum("ksu,kvw->ksuvw", first_im, second_im, precision=high)
    outer_im = jnp.einsum("ksu,kvw->ksuvw", first_re, second_im, precision=high) + jnp.einsum("ksu,kvw->ksuvw", first_im, second_re, precision=high)
    spin_re = spin_all[:, :, 0]
    spin_im = spin_all[:, :, 1]
    form = "ksuvw,xyuvws->kxy"
    block_re = jnp.einsum(form, outer_re, spin_re, precision=high) - jnp.einsum(form, outer_im, spin_im, precision=high)
    block_im = jnp.einsum(form, outer_re, spin_im, precision=high) + jnp.einsum(form, outer_im, spin_re, precision=high)
    return jnp.stack([block_re, block_im])


def reference(src_elem, snk_elem, peramb, insertions):
    signs = sign_vector(src_elem.shape[-1])

    def per_source(packed):
        source, peramb_row = packed

        def per_sink(inner):
            sink, pair = inner
            forward = forward_rows(source, pair)
            backward = backward_rows(sink, pair, signs)
            return spin_block(forward, backward)

        return lax.map(per_sink, (snk_elem, peramb_row))

    spin_all = lax.map(per_source, (src_elem, peramb))
    return insert_gammas(spin_all, insertions)
```

```python
import functools

import jax
import jax.numpy as jnp
import numpy as np
from jax import lax
from jax.experimental import pallas as pl
from jax.experimental.pallas import tpu as pltpu
from jax.sharding import PartitionSpec as P

MESH = pl.DeviceIdType.MESH
HIGH = lax.Precision.HIGHEST
SUB = 16


def gamma_tables():
    pauli = [
        np.array([[0, 1], [1, 0]], complex),
        np.array([[0, -1j], [1j, 0]], complex),
        np.array([[1, 0], [0, -1]], complex),
    ]
    basis = []
    for sigma in pauli:
        part = np.zeros((4, 4), complex)
        part[0:2, 2:4] = -1j * sigma
        part[2:4, 0:2] = 1j * sigma
        basis.append(part)
    fourth = np.zeros((4, 4), complex)
    fourth[0:2, 2:4] = np.eye(2)
    fourth[2:4, 0:2] = np.eye(2)
    basis.append(fourth)
    tables = []
    for subset in range(16):
        prod = np.eye(4, dtype=complex)
        for bit_index in range(4):
            if subset >> bit_index & 1:
                prod = prod @ basis[bit_index]
        tables.append(prod)
    return np.stack(tables)


def insertion_tables(sinks):
    gam = gamma_tables()
    parts = (gam.real, gam.imag)
    second = np.zeros((16, 2, 2, 4, 4, 4, 4, 2, 2), np.float32)
    first = np.zeros((16, 2, 2, 2, 4, 128), np.float32)
    for part in range(2):
        for c in range(2):
            for u in range(4):
                second[:, part, c, u, :, u, :, c, :] = parts[part].transpose(0, 2, 1)[..., None]
                for out in range(2):
                    for sink in range(sinks):
                        for s in range(4):
                            for d in range(2):
                                own = (part + c + d + out) % 2
                                sign = (-1.0) ** ((own + part + c + d - out) // 2)
                                first[:, out, part, c, u, sink * 8 + s * 2 + d] = sign * parts[own][:, s, u]
    return second.reshape(16, 4096), first.reshape(16, 4096)


def split(value):
    high = value.astype(jnp.bfloat16)
    low = (value - high.astype(jnp.float32)).astype(jnp.bfloat16)
    return high, low


def dot_trans(left, right):
    return lax.dot_general(left, right, (((1,), (1,)), ((), ())), preferred_element_type=jnp.float32)


def kernel(
    rows, cols, src_ref, snk_ref, per_ref, ins_ref, second_ref, first_ref, out_ref,
    src_all, snk_all, per, per_g, lhs, rhs, diag, second, first, sel_second, sel_first,
    local_sem, src_send, src_recv, snk_send, snk_recv,
):
    row, col = lax.axis_index("row"), lax.axis_index("col")
    sinks = per.shape[0]
    order = per.shape[-1]
    evecs = order // 4
    groups = evecs // SUB
    src_rows = src_all.shape[2]
    snk_rows = snk_all.shape[3]

    barrier = pltpu.get_barrier_semaphore()
    for step in range(1, cols):
        pl.semaphore_signal(
            barrier, inc=1, device_id={"col": lax.rem(col + step, cols)}, device_id_type=MESH
        )

    @pl.when(row > 0)
    def _():
        pl.semaphore_signal(barrier, inc=1, device_id={"row": row - 1}, device_id_type=MESH)

    @pl.when(row < rows - 1)
    def _():
        pl.semaphore_signal(barrier, inc=1, device_id={"row": row + 1}, device_id_type=MESH)

    locals_ = [
        pltpu.make_async_copy(per_ref.at[0], per, local_sem.at[0]),
        pltpu.make_async_copy(src_ref.at[0], src_all.at[col], local_sem.at[1]),
        pltpu.make_async_copy(snk_ref, snk_all.at[row], local_sem.at[2]),
        pltpu.make_async_copy(second_ref, second, local_sem.at[3]),
        pltpu.make_async_copy(first_ref, first, local_sem.at[4]),
    ]
    for copy in locals_:
        copy.start()

    neighbours = (row + rows - 1) // rows + (2 * rows - 2 - row) // rows
    pl.semaphore_wait(barrier, cols - 1 + neighbours)

    def hop(shard, sink, way, source):
        return pltpu.make_async_remote_copy(
            src_ref=source,
            dst_ref=snk_all.at[shard, sink],
            send_sem=snk_send.at[way, shard, sink],
            recv_sem=snk_recv.at[shard, sink],
            device_id={"row": row + 1 - 2 * way},
            device_id_type=MESH,
        )

    for sink in range(sinks):

        @pl.when(row < rows - 1)
        def _():
            hop(row, sink, 0, snk_ref.at[sink]).start()

        @pl.when(row > 0)
        def _():
            hop(row, sink, 1, snk_ref.at[sink]).start()

    def spread(step):
        return pltpu.make_async_remote_copy(
            src_ref=src_ref.at[0],
            dst_ref=src_all.at[col],
            send_sem=src_send.at[step],
            recv_sem=src_recv.at[col],
            device_id={"col": lax.rem(col + step, cols)},
            device_id_type=MESH,
        )

    for step in range(1, cols):
        spread(step).start()

    def arrive(step, sink):
        below, above = row - 1 - step, row + 1 + step

        @pl.when(below >= 0)
        def _():
            hop(below, sink, 0, snk_all.at[below, sink]).wait_recv()

            @pl.when(row < rows - 1)
            def _():
                hop(below, sink, 0, snk_all.at[below, sink]).start()

        @pl.when(above < rows)
        def _():
            hop(above, sink, 1, snk_all.at[above, sink]).wait_recv()

            @pl.when(row > 0)
            def _():
                hop(above, sink, 1, snk_all.at[above, sink]).start()

    for copy in locals_:
        copy.wait()

    lanes = lax.broadcasted_iota(jnp.int32, (1, order), 1)
    signs = jnp.where(lanes < 2 * evecs, 1.0, -1.0).astype(jnp.bfloat16)

    def sign_sink(sink, carry):
        for c in range(2):
            per_g[sink, c] = per[sink, c] * signs
        return carry

    lax.fori_loop(0, sinks, sign_sink, 0)

    codes = lax.broadcasted_iota(jnp.int32, (16, 16), 0)

    def chosen(which, table):
        onehot = jnp.where(codes == ins_ref[which : which + 1, :], 1.0, 0.0).astype(jnp.bfloat16)
        return lax.dot_general(
            onehot, table[...], (((0,), (0,)), ((), ())), preferred_element_type=jnp.float32
        )

    pick = chosen(1, second)
    for block in range(16):
        sel_second[block * 16 : (block + 1) * 16, :] = pick[:, block * 256 : (block + 1) * 256]
    sel_first[...] = chosen(0, first)

    def forward_sink(sink, carry):
        for shard in range(cols):
            u, first_group = divmod(shard * src_rows, evecs)
            first_group //= SUB
            pair = src_all[shard].reshape(2 * src_rows, order)
            with_re = jnp.dot(pair, per[sink, 0], preferred_element_type=jnp.float32)
            with_im = jnp.dot(pair, per[sink, 1], preferred_element_type=jnp.float32)
            both = (
                with_re[:src_rows] - with_im[src_rows:],
                with_im[:src_rows] + with_re[src_rows:],
            )
            for c in range(2):
                for h, piece in enumerate(split(both[c])):
                    for v in range(4):
                        for near in range(src_rows // SUB):
                            g = first_group + near
                            lhs[sink, u, v, c, h, :, g * evecs : (g + 1) * evecs] = piece[
                                near * SUB : (near + 1) * SUB, v * evecs : (v + 1) * evecs
                            ]
        return carry

    width = 16 * SUB
    same = lax.broadcasted_iota(jnp.int32, (SUB, width), 0) == lax.rem(
        lax.broadcasted_iota(jnp.int32, (SUB, width), 1), SUB
    )
    mask = jnp.where(same, 1.0, 0.0).astype(jnp.float32)

    def contract(sink, w, pair):
        with_re = dot_trans(per_g[sink, 0], pair)
        with_im = dot_trans(per_g[sink, 1], pair)
        both = (
            with_re[:, :evecs] + with_im[:, evecs:],
            with_re[:, evecs:] - with_im[:, :evecs],
        )
        for c in range(2):
            for h, piece in enumerate(split(both[c])):
                for s in range(4):
                    for g in range(groups):
                        start = s * evecs + g * SUB
                        rhs[s, c, h, :, g * evecs : (g + 1) * evecs] = piece[start : start + SUB]
        right = rhs[...].reshape(width, groups * evecs)
        for u in range(4):
            left = lhs[sink, u].reshape(width, groups * evecs)
            full = dot_trans(left, right).reshape(16, SUB, width)
            diag[sink, w, u * 16 : (u + 1) * 16, :] = jnp.sum(full * mask[None], axis=1)

    def whole_shard(shard, sink):
        contract(sink, shard, snk_all[shard, sink].reshape(2 * evecs, order))

    def both_ways(step, sink):
        def one(way, carry):
            shard = row + (2 * way - 1) * (1 + step)

            @pl.when(jnp.logical_and(shard >= 0, shard < rows))
            def _():
                whole_shard(shard, sink)

            return carry

        lax.fori_loop(0, 2, one, 0)

    def wait_sources():
        for step in range(1, cols):
            other = lax.rem(col + step, cols)
            pltpu.make_async_remote_copy(
                src_ref=src_ref.at[0],
                dst_ref=src_all.at[other],
                send_sem=src_send.at[step],
                recv_sem=src_recv.at[other],
                device_id={"col": other},
                device_id_type=MESH,
            ).wait_recv()

    if snk_rows == evecs:
        for sink in range(sinks):
            arrive(0, sink)
        wait_sources()
        lax.fori_loop(0, sinks, forward_sink, 0)

        def own(sink, carry):
            whole_shard(row, sink)
            return carry

        lax.fori_loop(0, sinks, own, 0)
        for step in range(1, rows - 1):
            for sink in range(sinks):
                arrive(step, sink)
                if step < rows - 2:
                    both_ways(step - 1, sink)
                else:
                    if sink == 0:
                        lax.fori_loop(
                            0, sinks, lambda k, carry: (both_ways(step - 1, k), carry)[1], 0
                        )
                    both_ways(step, sink)
    else:
        def pass_on(step, carry):
            for sink in range(sinks):
                arrive(step, sink)
            return carry

        lax.fori_loop(0, rows - 1, pass_on, 0)
        wait_sources()
        lax.fori_loop(0, sinks, forward_sink, 0)
        many = evecs // snk_rows

        def gathered(index, carry):
            sink, w = index // 4, lax.rem(index, 4)
            pieces = [snk_all[w * many + near, sink, c] for c in range(2) for near in range(many)]
            contract(sink, w, jnp.concatenate(pieces, axis=0))
            return carry

        lax.fori_loop(0, 4 * sinks, gathered, 0)

    at = lax.broadcasted_iota(jnp.int32, (width, 128), 0)
    to = lax.broadcasted_iota(jnp.int32, (width, 128), 1)
    fits = jnp.logical_and(at // 64 == lax.rem(to, 8) // 2, lax.rem(at // 32, 2) == lax.rem(to, 2))
    signed = jnp.where(fits, jnp.where(at < 128, 1.0, -1.0), 0.0).astype(jnp.float32)
    spins = jnp.zeros((256, 128), jnp.float32)
    for sink in range(sinks):
        place = jnp.where(to // 8 == sink, signed, 0.0)
        spins += jnp.dot(
            diag[sink].reshape(256, width), place, precision=HIGH, preferred_element_type=jnp.float32
        )
    mixed = jnp.dot(sel_second[...], spins, precision=HIGH, preferred_element_type=jnp.float32)
    lane = lax.broadcasted_iota(jnp.int32, (16, 128), 1)
    spot = lax.broadcasted_iota(jnp.int32, (16, sinks), 1)
    for out in range(2):
        total = jnp.zeros((16, 128), jnp.float32)
        for block in range(16):
            start = (out * 16 + block) * 128
            total += sel_first[:, start : start + 128] * mixed[block * 16 : (block + 1) * 16]
        result = jnp.zeros((16, sinks), jnp.float32)
        for sink in range(sinks):
            one = jnp.sum(jnp.where(lane // 8 == sink, total, 0.0), axis=1, keepdims=True)
            result = jnp.where(spot == sink, one, result)
        out_ref[out] = result

    for step in range(1, cols):
        spread(step).wait_send()

    def sent(shard, carry):
        for sink in range(sinks):

            @pl.when(jnp.logical_and(shard <= row, row < rows - 1))
            def _():
                hop(shard, sink, 0, snk_all.at[shard, sink]).wait_send()

            @pl.when(jnp.logical_and(shard >= row, row > 0))
            def _():
                hop(shard, sink, 1, snk_all.at[shard, sink]).wait_send()

        return carry

    lax.fori_loop(0, rows, sent, 0)


def shards(rows, cols, src_elem, snk_elem, peramb, insertions):
    sinks, order = peramb.shape[1], peramb.shape[-1]
    assert src_elem.shape[0] == 1 and sinks <= 16
    second, first = (jnp.asarray(table, jnp.bfloat16) for table in insertion_tables(sinks))
    anywhere = pl.BlockSpec(memory_space=pl.ANY)
    vmem = pl.BlockSpec(memory_space=pltpu.VMEM)
    half = jnp.bfloat16
    wide = order * 2
    blocks = pl.pallas_call(
        functools.partial(kernel, rows, cols),
        out_shape=jax.ShapeDtypeStruct((2, 16, sinks), jnp.float32),
        in_specs=[anywhere, anywhere, anywhere, vmem, anywhere, anywhere],
        out_specs=vmem,
        scratch_shapes=[
            pltpu.VMEM((cols,) + src_elem.shape[1:], half),
            pltpu.VMEM((rows,) + snk_elem.shape, half),
            pltpu.VMEM(peramb.shape[1:], half),
            pltpu.VMEM(peramb.shape[1:], half),
            pltpu.VMEM((sinks, 4, 4, 2, 2, SUB, wide), half),
            pltpu.VMEM((4, 2, 2, SUB, wide), half),
            pltpu.VMEM((sinks, 4, 64, 16 * SUB), jnp.float32),
            pltpu.VMEM((16, 4096), half),
            pltpu.VMEM((16, 4096), half),
            pltpu.VMEM((256, 256), jnp.float32),
            pltpu.VMEM((16, 4096), jnp.float32),
            pltpu.SemaphoreType.DMA((5,)),
            pltpu.SemaphoreType.DMA((cols,)),
            pltpu.SemaphoreType.DMA((cols,)),
            pltpu.SemaphoreType.DMA((2, rows, sinks)),
            pltpu.SemaphoreType.DMA((rows, sinks)),
        ],
        compiler_params=pltpu.CompilerParams(
            collective_id=0, has_side_effects=True, vmem_limit_bytes=40 * 1024 * 1024
        ),
    )(src_elem, snk_elem, peramb, insertions, second, first)
    return blocks[:, :, None, :]


def solution(mesh):
    placed = (
        P("row", "grp", "col", None),
        P("col", "grp", "row", None),
        P("row", "col", "grp", None, None),
        P(),
    )
    body = functools.partial(shards, mesh.shape["row"], mesh.shape["col"])
    return jax.shard_map(
        body, mesh=mesh, in_specs=placed, out_specs=P(None, "grp", "row", "col"), check_vma=False
    )
```

```python
import functools

import jax
import jax.numpy as jnp
import numpy as np
from jax import lax
from jax.experimental import pallas as pl
from jax.experimental.pallas import tpu as pltpu
from jax.sharding import PartitionSpec as P

MESH = pl.DeviceIdType.MESH
SUB = 16


def gamma_tables():
    pauli = [
        np.array([[0, 1], [1, 0]], complex),
        np.array([[0, -1j], [1j, 0]], complex),
        np.array([[1, 0], [0, -1]], complex),
    ]
    basis = []
    for sigma in pauli:
        part = np.zeros((4, 4), complex)
        part[0:2, 2:4] = -1j * sigma
        part[2:4, 0:2] = 1j * sigma
        basis.append(part)
    fourth = np.zeros((4, 4), complex)
    fourth[0:2, 2:4] = np.eye(2)
    fourth[2:4, 0:2] = np.eye(2)
    basis.append(fourth)
    tables = []
    for subset in range(16):
        prod = np.eye(4, dtype=complex)
        for bit_index in range(4):
            if subset >> bit_index & 1:
                prod = prod @ basis[bit_index]
        tables.append(prod)
    return np.stack(tables)


def insertion_tables(sinks):
    gam = gamma_tables()
    parts = (gam.real, gam.imag)
    second = np.zeros((16, 2, 2, 4, 4, 4, 4, 2, 2), np.float32)
    first = np.zeros((16, 2, 2, 2, 4, 128), np.float32)
    for part in range(2):
        for c in range(2):
            for u in range(4):
                second[:, part, c, u, :, u, :, c, :] = parts[part].transpose(0, 2, 1)[..., None]
                for out in range(2):
                    for sink in range(sinks):
                        for s in range(4):
                            for d in range(2):
                                own = (part + c + d + out) % 2
                                sign = (-1.0) ** ((own + part + c + d - out) // 2)
                                first[:, out, part, c, u, sink * 8 + s * 2 + d] = sign * parts[own][:, s, u]
    return second.reshape(16, 4096), first.reshape(16, 4096)


def split(value):
    high = value.astype(jnp.bfloat16)
    low = (value - high.astype(jnp.float32)).astype(jnp.bfloat16)
    return high, low


def dot_trans(left, right):
    return lax.dot_general(left, right, (((1,), (1,)), ((), ())), preferred_element_type=jnp.float32)


def kernel(
    rows, cols, src_ref, snk_ref, per_ref, ins_ref, second_ref, first_ref, out_ref,
    src_all, snk_all, per, per_g, lhs, rhs, spins, ins, second, first, sel_second, sel_first,
    local_sem, src_send, src_recv, snk_send, snk_recv,
):
    row, col = lax.axis_index("row"), lax.axis_index("col")
    sinks = per.shape[0]
    order = per.shape[-1]
    evecs = order // 4
    groups = evecs // SUB
    src_rows = src_all.shape[2]
    snk_rows = snk_all.shape[3]

    barrier = pltpu.get_barrier_semaphore()
    for step in range(1, cols):
        pl.semaphore_signal(
            barrier, inc=1, device_id={"col": lax.rem(col + step, cols)}, device_id_type=MESH
        )

    @pl.when(row > 0)
    def _():
        pl.semaphore_signal(barrier, inc=1, device_id={"row": row - 1}, device_id_type=MESH)

    @pl.when(row < rows - 1)
    def _():
        pl.semaphore_signal(barrier, inc=1, device_id={"row": row + 1}, device_id_type=MESH)

    locals_ = [
        pltpu.make_async_copy(per_ref.at[0], per, local_sem.at[0]),
        pltpu.make_async_copy(src_ref.at[0], src_all.at[col], local_sem.at[1]),
        pltpu.make_async_copy(snk_ref, snk_all.at[row], local_sem.at[2]),
        pltpu.make_async_copy(second_ref, second, local_sem.at[3]),
        pltpu.make_async_copy(first_ref, first, local_sem.at[4]),
        pltpu.make_async_copy(ins_ref, ins, local_sem.at[5]),
    ]
    for copy in locals_:
        copy.start()

    neighbours = (row + rows - 1) // rows + (2 * rows - 2 - row) // rows
    pl.semaphore_wait(barrier, cols - 1 + neighbours)

    def hop(shard, sink, way, source):
        return pltpu.make_async_remote_copy(
            src_ref=source,
            dst_ref=snk_all.at[shard, sink],
            send_sem=snk_send.at[way, shard, sink],
            recv_sem=snk_recv.at[shard, sink],
            device_id={"row": row + 1 - 2 * way},
            device_id_type=MESH,
        )

    for sink in range(sinks):

        @pl.when(row < rows - 1)
        def _():
            hop(row, sink, 0, snk_ref.at[sink]).start()

        @pl.when(row > 0)
        def _():
            hop(row, sink, 1, snk_ref.at[sink]).start()

    def spread(step):
        return pltpu.make_async_remote_copy(
            src_ref=src_ref.at[0],
            dst_ref=src_all.at[col],
            send_sem=src_send.at[step],
            recv_sem=src_recv.at[col],
            device_id={"col": lax.rem(col + step, cols)},
            device_id_type=MESH,
        )

    for step in range(1, cols):
        spread(step).start()

    def arrive(step, sink):
        below, above = row - 1 - step, row + 1 + step

        @pl.when(below >= 0)
        def _():
            hop(below, sink, 0, snk_all.at[below, sink]).wait_recv()

            @pl.when(row < rows - 1)
            def _():
                hop(below, sink, 0, snk_all.at[below, sink]).start()

        @pl.when(above < rows)
        def _():
            hop(above, sink, 1, snk_all.at[above, sink]).wait_recv()

            @pl.when(row > 0)
            def _():
                hop(above, sink, 1, snk_all.at[above, sink]).start()

    for copy in locals_:
        copy.wait()

    lanes = lax.broadcasted_iota(jnp.int32, (1, order), 1)
    signs = jnp.where(lanes < 2 * evecs, 1.0, -1.0).astype(jnp.bfloat16)

    def sign_sink(sink, carry):
        for c in range(2):
            per_g[sink, c] = per[sink, c] * signs
        return carry

    lax.fori_loop(0, sinks, sign_sink, 0)

    codes = lax.broadcasted_iota(jnp.int32, (16, 16), 0)

    def chosen(which, table):
        onehot = jnp.where(codes == ins[which : which + 1, :], 1.0, 0.0).astype(jnp.bfloat16)
        return lax.dot_general(
            onehot, table[...].astype(jnp.bfloat16), (((0,), (0,)), ((), ())), preferred_element_type=jnp.float32
        )

    pick = chosen(1, second)
    for block in range(16):
        sel_second[block * 16 : (block + 1) * 16, :] = pick[
            :, block * 256 : (block + 1) * 256
        ].astype(jnp.bfloat16)
    sel_first[...] = chosen(0, first)

    def forward_sink(sink, carry):
        for shard in range(cols):
            u, first_group = divmod(shard * src_rows, evecs)
            first_group //= SUB
            pair = src_all[shard].reshape(2 * src_rows, order)
            with_re = jnp.dot(pair, per[sink, 0], preferred_element_type=jnp.float32)
            with_im = jnp.dot(pair, per[sink, 1], preferred_element_type=jnp.float32)
            both = (
                with_re[:src_rows] - with_im[src_rows:],
                with_im[:src_rows] + with_re[src_rows:],
            )
            for c in range(2):
                for h, piece in enumerate(split(both[c])):
                    for v in range(4):
                        for near in range(src_rows // SUB):
                            g = first_group + near
                            lhs[sink, u, v, c, h, :, g * evecs : (g + 1) * evecs] = piece[
                                near * SUB : (near + 1) * SUB, v * evecs : (v + 1) * evecs
                            ]
        return carry

    width = 16 * SUB
    same = lax.broadcasted_iota(jnp.int32, (SUB, width), 0) == lax.rem(
        lax.broadcasted_iota(jnp.int32, (SUB, width), 1), SUB
    )
    mask = jnp.where(same, 1.0, 0.0).astype(jnp.float32)

    at = lax.broadcasted_iota(jnp.int32, (width, 128), 0)
    to = lax.broadcasted_iota(jnp.int32, (width, 128), 1)
    fits = jnp.logical_and(at // 64 == lax.rem(to, 8) // 2, lax.rem(at // 32, 2) == lax.rem(to, 2))
    signed = jnp.where(fits, jnp.where(at < 128, 1.0, -1.0), 0.0).astype(jnp.float32)
    spins[...] = jnp.zeros_like(spins)

    def contract(sink, w, pair):
        with_re = dot_trans(per_g[sink, 0], pair)
        with_im = dot_trans(per_g[sink, 1], pair)
        both = (
            with_re[:, :evecs] + with_im[:, evecs:],
            with_re[:, evecs:] - with_im[:, :evecs],
        )
        for c in range(2):
            for h, piece in enumerate(split(both[c])):
                for s in range(4):
                    for g in range(groups):
                        start = s * evecs + g * SUB
                        rhs[s, c, h, :, g * evecs : (g + 1) * evecs] = piece[start : start + SUB]
        right = rhs[...].reshape(width, groups * evecs)
        sums = []
        for u in range(4):
            left = lhs[sink, u].reshape(width, groups * evecs)
            full = dot_trans(left, right).reshape(16, SUB, width)
            sums.append(jnp.sum(full * mask[None], axis=1))
        place = jnp.where(to // 8 == sink, signed, 0.0).astype(jnp.bfloat16)
        pair = jnp.concatenate(split(jnp.concatenate(sums, axis=0)), axis=1)
        spins[w] += jnp.dot(
            pair, jnp.concatenate([place, place], axis=0), preferred_element_type=jnp.float32
        )

    def whole_shard(shard, sink):
        contract(sink, shard, snk_all[shard, sink].reshape(2 * evecs, order))

    def both_ways(step, sink):
        def one(way, carry):
            shard = row + (2 * way - 1) * (1 + step)

            @pl.when(jnp.logical_and(shard >= 0, shard < rows))
            def _():
                whole_shard(shard, sink)

            return carry

        lax.fori_loop(0, 2, one, 0)

    def wait_sources():
        for step in range(1, cols):
            other = lax.rem(col + step, cols)
            pltpu.make_async_remote_copy(
                src_ref=src_ref.at[0],
                dst_ref=src_all.at[other],
                send_sem=src_send.at[step],
                recv_sem=src_recv.at[other],
                device_id={"col": other},
                device_id_type=MESH,
            ).wait_recv()

    if snk_rows == evecs:
        for sink in range(sinks):
            arrive(0, sink)
        wait_sources()
        lax.fori_loop(0, sinks, forward_sink, 0)

        def own(sink, carry):
            whole_shard(row, sink)
            return carry

        lax.fori_loop(0, sinks, own, 0)
        for step in range(1, rows - 1):
            for sink in range(sinks):
                arrive(step, sink)
                if step < rows - 2:
                    both_ways(step - 1, sink)
                else:
                    if sink == 0:
                        lax.fori_loop(
                            0, sinks, lambda k, carry: (both_ways(step - 1, k), carry)[1], 0
                        )
                    both_ways(step, sink)
    else:
        def pass_on(step, carry):
            for sink in range(sinks):
                arrive(step, sink)
            return carry

        lax.fori_loop(0, rows - 1, pass_on, 0)
        wait_sources()
        lax.fori_loop(0, sinks, forward_sink, 0)
        many = evecs // snk_rows

        def gathered(index, carry):
            sink, w = index // 4, lax.rem(index, 4)
            pieces = [snk_all[w * many + near, sink, c] for c in range(2) for near in range(many)]
            contract(sink, w, jnp.concatenate(pieces, axis=0))
            return carry

        lax.fori_loop(0, 4 * sinks, gathered, 0)

    halves = jnp.concatenate(split(spins[...].reshape(256, 128)), axis=1)
    mixed = jnp.dot(sel_second[...], halves, preferred_element_type=jnp.float32)
    mixed = mixed[:, :128] + mixed[:, 128:]
    totals = []
    for out in range(2):
        total = jnp.zeros((16, 128), jnp.float32)
        for block in range(16):
            start = (out * 16 + block) * 128
            total += sel_first[:, start : start + 128] * mixed[block * 16 : (block + 1) * 16]
        totals.append(total)
    sink_of = lax.broadcasted_iota(jnp.int32, (16, 128), 1) // 8
    member = jnp.where(sink_of == lax.broadcasted_iota(jnp.int32, (16, 128), 0), 1.0, 0.0)
    ends = dot_trans(
        member.astype(jnp.bfloat16), jnp.concatenate(split(jnp.concatenate(totals, axis=0)), axis=0)
    )
    ends = ends[:, :32] + ends[:, 32:]
    for out in range(2):
        out_ref[out] = ends[:sinks, out * 16 : (out + 1) * 16]

    for step in range(1, cols):
        spread(step).wait_send()

    def sent(shard, carry):
        for sink in range(sinks):

            @pl.when(jnp.logical_and(shard <= row, row < rows - 1))
            def _():
                hop(shard, sink, 0, snk_all.at[shard, sink]).wait_send()

            @pl.when(jnp.logical_and(shard >= row, row > 0))
            def _():
                hop(shard, sink, 1, snk_all.at[shard, sink]).wait_send()

        return carry

    lax.fori_loop(0, rows, sent, 0)


def shards(rows, cols, src_elem, snk_elem, peramb, insertions):
    sinks, order = peramb.shape[1], peramb.shape[-1]
    assert src_elem.shape[0] == 1 and sinks <= 16
    second, first = (jnp.asarray(table, jnp.float32) for table in insertion_tables(sinks))
    anywhere = pl.BlockSpec(memory_space=pltpu.HBM)
    vmem = pl.BlockSpec(memory_space=pltpu.VMEM)
    half = jnp.bfloat16
    wide = order * 2
    blocks = pl.pallas_call(
        functools.partial(kernel, rows, cols),
        out_shape=jax.ShapeDtypeStruct((2, sinks, 16), jnp.float32),
        in_specs=[anywhere] * 6,
        out_specs=vmem,
        scratch_shapes=[
            pltpu.VMEM((cols,) + src_elem.shape[1:], half),
            pltpu.VMEM((rows,) + snk_elem.shape, half),
            pltpu.VMEM(peramb.shape[1:], half),
            pltpu.VMEM(peramb.shape[1:], half),
            pltpu.VMEM((sinks, 4, 4, 2, 2, SUB, wide), half),
            pltpu.VMEM((4, 2, 2, SUB, wide), half),
            pltpu.VMEM((4, 64, 128), jnp.float32),
            pltpu.VMEM(insertions.shape, jnp.int32),
            pltpu.VMEM((16, 4096), jnp.float32),
            pltpu.VMEM((16, 4096), jnp.float32),
            pltpu.VMEM((256, 256), half),
            pltpu.VMEM((16, 4096), jnp.float32),
            pltpu.SemaphoreType.DMA((6,)),
            pltpu.SemaphoreType.DMA((cols,)),
            pltpu.SemaphoreType.DMA((cols,)),
            pltpu.SemaphoreType.DMA((2, rows, sinks)),
            pltpu.SemaphoreType.DMA((rows, sinks)),
        ],
        compiler_params=pltpu.CompilerParams(
            collective_id=0, has_side_effects=True, vmem_limit_bytes=64 * 1024 * 1024
        ),
    )(src_elem, snk_elem, peramb, insertions, second, first)
    return blocks.transpose(0, 2, 1)[:, :, None, :]


def solution(mesh):
    placed = (
        P("row", "grp", "col", None),
        P("col", "grp", "row", None),
        P("row", "col", "grp", None, None),
        P(),
    )
    body = functools.partial(shards, mesh.shape["row"], mesh.shape["col"])
    return jax.shard_map(
        body, mesh=mesh, in_specs=placed, out_specs=P(None, "grp", "row", "col"), check_vma=False
    )
```

```python
import functools

import jax
import jax.numpy as jnp
import numpy as np
from jax import lax
from jax.experimental import pallas as pl
from jax.experimental.pallas import tpu as pltpu
from jax.sharding import PartitionSpec as P

MESH = pl.DeviceIdType.MESH
SUB = 16


def gamma_tables():
    pauli = [
        np.array([[0, 1], [1, 0]], complex),
        np.array([[0, -1j], [1j, 0]], complex),
        np.array([[1, 0], [0, -1]], complex),
    ]
    basis = []
    for sigma in pauli:
        part = np.zeros((4, 4), complex)
        part[0:2, 2:4] = -1j * sigma
        part[2:4, 0:2] = 1j * sigma
        basis.append(part)
    fourth = np.zeros((4, 4), complex)
    fourth[0:2, 2:4] = np.eye(2)
    fourth[2:4, 0:2] = np.eye(2)
    basis.append(fourth)
    tables = []
    for subset in range(16):
        prod = np.eye(4, dtype=complex)
        for bit_index in range(4):
            if subset >> bit_index & 1:
                prod = prod @ basis[bit_index]
        tables.append(prod)
    return np.stack(tables)


def insertion_tables(sinks):
    gam = gamma_tables()
    parts = (gam.real, gam.imag)
    second = np.zeros((16, 2, 2, 4, 4, 4, 4, 2, 2), np.float32)
    first = np.zeros((16, 2, 2, 2, 4, 128), np.float32)
    for part in range(2):
        for c in range(2):
            for u in range(4):
                second[:, part, c, u, :, u, :, c, :] = parts[part].transpose(0, 2, 1)[..., None]
                for out in range(2):
                    for sink in range(sinks):
                        for s in range(4):
                            for d in range(2):
                                own = (part + c + d + out) % 2
                                sign = (-1.0) ** ((own + part + c + d - out) // 2)
                                first[:, out, part, c, u, sink * 8 + s * 2 + d] = sign * parts[own][:, s, u]
    return second.reshape(16, 4096), first.reshape(16, 4096)


def split(value):
    high = value.astype(jnp.bfloat16)
    low = (value - high.astype(jnp.float32)).astype(jnp.bfloat16)
    return high, low


def dot_trans(left, right):
    return lax.dot_general(left, right, (((1,), (1,)), ((), ())), preferred_element_type=jnp.float32)


def kernel(
    rows, cols, src_ref, snk_ref, per_ref, ins_ref, second_ref, first_ref, out_ref,
    src_all, snk_all, per, per_g, lhs, rhs, spins, ins, second, first, sel_second, sel_first,
    local_sem, src_send, src_recv, snk_send, snk_recv,
):
    row, col = lax.axis_index("row"), lax.axis_index("col")
    sinks = per.shape[0]
    order = per.shape[-1]
    evecs = order // 4
    groups = evecs // SUB
    src_rows = src_all.shape[2]
    snk_rows = snk_all.shape[3]

    barrier = pltpu.get_barrier_semaphore()
    for step in range(1, cols):
        pl.semaphore_signal(
            barrier, inc=1, device_id={"col": lax.rem(col + step, cols)}, device_id_type=MESH
        )

    @pl.when(row > 0)
    def _():
        pl.semaphore_signal(barrier, inc=1, device_id={"row": row - 1}, device_id_type=MESH)

    @pl.when(row < rows - 1)
    def _():
        pl.semaphore_signal(barrier, inc=1, device_id={"row": row + 1}, device_id_type=MESH)

    locals_ = [
        pltpu.make_async_copy(per_ref.at[0], per, local_sem.at[0]),
        pltpu.make_async_copy(src_ref.at[0], src_all.at[col], local_sem.at[1]),
        pltpu.make_async_copy(snk_ref, snk_all.at[row], local_sem.at[2]),
        pltpu.make_async_copy(second_ref, second, local_sem.at[3]),
        pltpu.make_async_copy(first_ref, first, local_sem.at[4]),
        pltpu.make_async_copy(ins_ref, ins, local_sem.at[5]),
    ]
    for copy in locals_:
        copy.start()

    neighbours = (row + rows - 1) // rows + (2 * rows - 2 - row) // rows
    pl.semaphore_wait(barrier, cols - 1 + neighbours)

    def hop(shard, sink, way, source):
        return pltpu.make_async_remote_copy(
            src_ref=source,
            dst_ref=snk_all.at[shard, sink],
            send_sem=snk_send.at[way, shard, sink],
            recv_sem=snk_recv.at[shard, sink],
            device_id={"row": row + 1 - 2 * way},
            device_id_type=MESH,
        )

    near = 2 * row // rows
    for turn in range(2):
        for sink in range(sinks):
            for way in range(2):
                there = row < rows - 1 if way == 0 else row > 0

                @pl.when(jnp.logical_and(there, (near + way + turn) % 2 == 1))
                def _():
                    hop(row, sink, way, snk_ref.at[sink]).start()

    def spread(step):
        return pltpu.make_async_remote_copy(
            src_ref=src_ref.at[0],
            dst_ref=src_all.at[col],
            send_sem=src_send.at[step],
            recv_sem=src_recv.at[col],
            device_id={"col": lax.rem(col + step, cols)},
            device_id_type=MESH,
        )

    for step in range(1, cols):
        spread(step).start()

    def arrive(step, sink):
        below, above = row - 1 - step, row + 1 + step

        @pl.when(below >= 0)
        def _():
            hop(below, sink, 0, snk_all.at[below, sink]).wait_recv()

            @pl.when(row < rows - 1)
            def _():
                hop(below, sink, 0, snk_all.at[below, sink]).start()

        @pl.when(above < rows)
        def _():
            hop(above, sink, 1, snk_all.at[above, sink]).wait_recv()

            @pl.when(row > 0)
            def _():
                hop(above, sink, 1, snk_all.at[above, sink]).start()

    for copy in locals_:
        copy.wait()

    lanes = lax.broadcasted_iota(jnp.int32, (1, order), 1)
    signs = jnp.where(lanes < 2 * evecs, 1.0, -1.0).astype(jnp.bfloat16)

    def sign_sink(sink, carry):
        for c in range(2):
            per_g[sink, c] = per[sink, c] * signs
        return carry

    lax.fori_loop(0, sinks, sign_sink, 0)

    codes = lax.broadcasted_iota(jnp.int32, (16, 16), 0)

    def chosen(which, table):
        onehot = jnp.where(codes == ins[which : which + 1, :], 1.0, 0.0).astype(jnp.bfloat16)
        return lax.dot_general(
            onehot, table[...].astype(jnp.bfloat16), (((0,), (0,)), ((), ())), preferred_element_type=jnp.float32
        )

    pick = chosen(1, second)
    for block in range(16):
        sel_second[block * 16 : (block + 1) * 16, :] = pick[
            :, block * 256 : (block + 1) * 256
        ].astype(jnp.bfloat16)
    sel_first[...] = chosen(0, first)

    def forward_sink(sink, carry):
        for shard in range(cols):
            u, first_group = divmod(shard * src_rows, evecs)
            first_group //= SUB
            pair = src_all[shard].reshape(2 * src_rows, order)
            with_re = jnp.dot(pair, per[sink, 0], preferred_element_type=jnp.float32)
            with_im = jnp.dot(pair, per[sink, 1], preferred_element_type=jnp.float32)
            both = (
                with_re[:src_rows] - with_im[src_rows:],
                with_im[:src_rows] + with_re[src_rows:],
            )
            for c in range(2):
                for h, piece in enumerate(split(both[c])):
                    for v in range(4):
                        for near in range(src_rows // SUB):
                            g = first_group + near
                            lhs[sink, u, v, c, h, :, g * evecs : (g + 1) * evecs] = piece[
                                near * SUB : (near + 1) * SUB, v * evecs : (v + 1) * evecs
                            ]
        return carry

    width = 16 * SUB
    same = lax.broadcasted_iota(jnp.int32, (SUB, width), 0) == lax.rem(
        lax.broadcasted_iota(jnp.int32, (SUB, width), 1), SUB
    )
    mask = jnp.where(same, 1.0, 0.0).astype(jnp.float32)

    at = lax.broadcasted_iota(jnp.int32, (width, 128), 0)
    to = lax.broadcasted_iota(jnp.int32, (width, 128), 1)
    fits = jnp.logical_and(at // 64 == lax.rem(to, 8) // 2, lax.rem(at // 32, 2) == lax.rem(to, 2))
    signed = jnp.where(fits, jnp.where(at < 128, 1.0, -1.0), 0.0).astype(jnp.float32)
    spins[...] = jnp.zeros_like(spins)

    def contract(sink, w, pair):
        with_re = dot_trans(per_g[sink, 0], pair)
        with_im = dot_trans(per_g[sink, 1], pair)
        both = (
            with_re[:, :evecs] + with_im[:, evecs:],
            with_re[:, evecs:] - with_im[:, :evecs],
        )
        for c in range(2):
            for h, piece in enumerate(split(both[c])):
                for s in range(4):
                    for g in range(groups):
                        start = s * evecs + g * SUB
                        rhs[s, c, h, :, g * evecs : (g + 1) * evecs] = piece[start : start + SUB]
        right = rhs[...].reshape(width, groups * evecs)
        sums = []
        for u in range(4):
            left = lhs[sink, u].reshape(width, groups * evecs)
            full = dot_trans(left, right).reshape(16, SUB, width)
            sums.append(jnp.sum(full * mask[None], axis=1))
        place = jnp.where(to // 8 == sink, signed, 0.0).astype(jnp.bfloat16)
        pair = jnp.concatenate(split(jnp.concatenate(sums, axis=0)), axis=1)
        spins[w] += jnp.dot(
            pair, jnp.concatenate([place, place], axis=0), preferred_element_type=jnp.float32
        )

    def whole_shard(shard, sink):
        contract(sink, shard, snk_all[shard, sink].reshape(2 * evecs, order))

    def both_ways(step, sink):
        def one(way, carry):
            shard = row + (2 * way - 1) * (1 + step)

            @pl.when(jnp.logical_and(shard >= 0, shard < rows))
            def _():
                whole_shard(shard, sink)

            return carry

        lax.fori_loop(0, 2, one, 0)

    def wait_sources():
        for step in range(1, cols):
            other = lax.rem(col + step, cols)
            pltpu.make_async_remote_copy(
                src_ref=src_ref.at[0],
                dst_ref=src_all.at[other],
                send_sem=src_send.at[step],
                recv_sem=src_recv.at[other],
                device_id={"col": other},
                device_id_type=MESH,
            ).wait_recv()

    if snk_rows == evecs:
        for sink in range(sinks):
            arrive(0, sink)
        wait_sources()
        lax.fori_loop(0, sinks, forward_sink, 0)

        def own(sink, carry):
            whole_shard(row, sink)
            return carry

        lax.fori_loop(0, sinks, own, 0)
        for step in range(1, rows - 2):
            for sink in range(sinks):
                arrive(step, sink)
                both_ways(step - 1, sink)
        for sink in range(sinks):
            if rows > 2:
                both_ways(rows - 3, sink)
        for sink in range(sinks):
            if rows > 2:
                arrive(rows - 2, sink)
            both_ways(rows - 2, sink)
    else:
        def pass_on(step, carry):
            for sink in range(sinks):
                arrive(step, sink)
            return carry

        lax.fori_loop(0, rows - 1, pass_on, 0)
        wait_sources()
        lax.fori_loop(0, sinks, forward_sink, 0)
        many = evecs // snk_rows

        def gathered(index, carry):
            sink, w = index // 4, lax.rem(index, 4)
            pieces = [snk_all[w * many + near, sink, c] for c in range(2) for near in range(many)]
            contract(sink, w, jnp.concatenate(pieces, axis=0))
            return carry

        lax.fori_loop(0, 4 * sinks, gathered, 0)

    halves = jnp.concatenate(split(spins[...].reshape(256, 128)), axis=1)
    mixed = jnp.dot(sel_second[...], halves, preferred_element_type=jnp.float32)
    mixed = mixed[:, :128] + mixed[:, 128:]
    totals = []
    for out in range(2):
        total = jnp.zeros((16, 128), jnp.float32)
        for block in range(16):
            start = (out * 16 + block) * 128
            total += sel_first[:, start : start + 128] * mixed[block * 16 : (block + 1) * 16]
        totals.append(total)
    sink_of = lax.broadcasted_iota(jnp.int32, (16, 128), 1) // 8
    member = jnp.where(sink_of == lax.broadcasted_iota(jnp.int32, (16, 128), 0), 1.0, 0.0)
    ends = dot_trans(
        member.astype(jnp.bfloat16), jnp.concatenate(split(jnp.concatenate(totals, axis=0)), axis=0)
    )
    ends = ends[:, :32] + ends[:, 32:]
    for out in range(2):
        out_ref[out] = ends[:sinks, out * 16 : (out + 1) * 16]

    for step in range(1, cols):
        spread(step).wait_send()

    def sent(shard, carry):
        for sink in range(sinks):

            @pl.when(jnp.logical_and(shard <= row, row < rows - 1))
            def _():
                hop(shard, sink, 0, snk_all.at[shard, sink]).wait_send()

            @pl.when(jnp.logical_and(shard >= row, row > 0))
            def _():
                hop(shard, sink, 1, snk_all.at[shard, sink]).wait_send()

        return carry

    lax.fori_loop(0, rows, sent, 0)


def shards(rows, cols, src_elem, snk_elem, peramb, insertions):
    sinks, order = peramb.shape[1], peramb.shape[-1]
    assert src_elem.shape[0] == 1 and sinks <= 16
    second, first = (jnp.asarray(table, jnp.float32) for table in insertion_tables(sinks))
    anywhere = pl.BlockSpec(memory_space=pltpu.HBM)
    vmem = pl.BlockSpec(memory_space=pltpu.VMEM)
    half = jnp.bfloat16
    wide = order * 2
    blocks = pl.pallas_call(
        functools.partial(kernel, rows, cols),
        out_shape=jax.ShapeDtypeStruct((2, sinks, 16), jnp.float32),
        in_specs=[anywhere] * 6,
        out_specs=vmem,
        scratch_shapes=[
            pltpu.VMEM((cols,) + src_elem.shape[1:], half),
            pltpu.VMEM((rows,) + snk_elem.shape, half),
            pltpu.VMEM(peramb.shape[1:], half),
            pltpu.VMEM(peramb.shape[1:], half),
            pltpu.VMEM((sinks, 4, 4, 2, 2, SUB, wide), half),
            pltpu.VMEM((4, 2, 2, SUB, wide), half),
            pltpu.VMEM((4, 64, 128), jnp.float32),
            pltpu.VMEM(insertions.shape, jnp.int32),
            pltpu.VMEM((16, 4096), jnp.float32),
            pltpu.VMEM((16, 4096), jnp.float32),
            pltpu.VMEM((256, 256), half),
            pltpu.VMEM((16, 4096), jnp.float32),
            pltpu.SemaphoreType.DMA((6,)),
            pltpu.SemaphoreType.DMA((cols,)),
            pltpu.SemaphoreType.DMA((cols,)),
            pltpu.SemaphoreType.DMA((2, rows, sinks)),
            pltpu.SemaphoreType.DMA((rows, sinks)),
        ],
        compiler_params=pltpu.CompilerParams(
            collective_id=0, has_side_effects=True, vmem_limit_bytes=64 * 1024 * 1024
        ),
    )(src_elem, snk_elem, peramb, insertions, second, first)
    return blocks.transpose(0, 2, 1)[:, :, None, :]


def solution(mesh):
    placed = (
        P("row", "grp", "col", None),
        P("col", "grp", "row", None),
        P("row", "col", "grp", None, None),
        P(),
    )
    body = functools.partial(shards, mesh.shape["row"], mesh.shape["col"])
    return jax.shard_map(
        body, mesh=mesh, in_specs=placed, out_specs=P(None, "grp", "row", "col"), check_vma=False
    )
```

```python
import functools

import jax
import jax.numpy as jnp
import numpy as np
from jax import lax
from jax.experimental import pallas as pl
from jax.experimental.pallas import tpu as pltpu
from jax.sharding import PartitionSpec as P

MESH = pl.DeviceIdType.MESH
SUB = 16


def gamma_tables():
    pauli = [
        np.array([[0, 1], [1, 0]], complex),
        np.array([[0, -1j], [1j, 0]], complex),
        np.array([[1, 0], [0, -1]], complex),
    ]
    basis = []
    for sigma in pauli:
        part = np.zeros((4, 4), complex)
        part[0:2, 2:4] = -1j * sigma
        part[2:4, 0:2] = 1j * sigma
        basis.append(part)
    fourth = np.zeros((4, 4), complex)
    fourth[0:2, 2:4] = np.eye(2)
    fourth[2:4, 0:2] = np.eye(2)
    basis.append(fourth)
    tables = []
    for subset in range(16):
        prod = np.eye(4, dtype=complex)
        for bit_index in range(4):
            if subset >> bit_index & 1:
                prod = prod @ basis[bit_index]
        tables.append(prod)
    return np.stack(tables)


def insertion_tables(sinks):
    gam = gamma_tables()
    parts = (gam.real, gam.imag)
    second = np.zeros((16, 2, 2, 4, 4, 4, 4, 2, 2), np.float32)
    first = np.zeros((16, 2, 2, 2, 4, 128), np.float32)
    for part in range(2):
        for c in range(2):
            for u in range(4):
                second[:, part, c, u, :, u, :, c, :] = parts[part].transpose(0, 2, 1)[..., None]
                for out in range(2):
                    for sink in range(sinks):
                        for s in range(4):
                            for d in range(2):
                                own = (part + c + d + out) % 2
                                sign = (-1.0) ** ((own + part + c + d - out) // 2)
                                first[:, out, part, c, u, sink * 8 + s * 2 + d] = sign * parts[own][:, s, u]
    return second.reshape(16, 4096), first.reshape(16, 4096)


def split(value):
    high = value.astype(jnp.bfloat16)
    low = (value - high.astype(jnp.float32)).astype(jnp.bfloat16)
    return high, low


def dot_trans(left, right):
    return lax.dot_general(left, right, (((1,), (1,)), ((), ())), preferred_element_type=jnp.float32)


def kernel(
    rows, cols, src_ref, snk_ref, per_ref, ins_ref, second_ref, first_ref, out_ref,
    src_all, snk_all, per, per_g, lhs, rhs, spins, ins, second, first, sel_second, sel_first,
    local_sem, src_send, src_recv, snk_send, snk_recv,
):
    row, col = lax.axis_index("row"), lax.axis_index("col")
    sinks = per.shape[0]
    order = per.shape[-1]
    evecs = order // 4
    groups = evecs // SUB
    src_rows = src_all.shape[2]
    snk_rows = snk_all.shape[3]

    barrier = pltpu.get_barrier_semaphore()
    for step in range(1, cols):
        pl.semaphore_signal(
            barrier, inc=1, device_id={"col": lax.rem(col + step, cols)}, device_id_type=MESH
        )

    @pl.when(row > 0)
    def _():
        pl.semaphore_signal(barrier, inc=1, device_id={"row": row - 1}, device_id_type=MESH)

    @pl.when(row < rows - 1)
    def _():
        pl.semaphore_signal(barrier, inc=1, device_id={"row": row + 1}, device_id_type=MESH)

    locals_ = [
        pltpu.make_async_copy(per_ref.at[0], per, local_sem.at[0]),
        pltpu.make_async_copy(src_ref.at[0], src_all.at[col], local_sem.at[1]),
        pltpu.make_async_copy(snk_ref, snk_all.at[row], local_sem.at[2]),
        pltpu.make_async_copy(second_ref, second, local_sem.at[3]),
        pltpu.make_async_copy(first_ref, first, local_sem.at[4]),
        pltpu.make_async_copy(ins_ref, ins, local_sem.at[5]),
    ]
    for copy in locals_:
        copy.start()

    neighbours = (row + rows - 1) // rows + (2 * rows - 2 - row) // rows
    pl.semaphore_wait(barrier, cols - 1 + neighbours)

    def hop(shard, sink, way, source):
        return pltpu.make_async_remote_copy(
            src_ref=source,
            dst_ref=snk_all.at[shard, sink],
            send_sem=snk_send.at[way, shard, sink],
            recv_sem=snk_recv.at[shard, sink],
            device_id={"row": row + 1 - 2 * way},
            device_id_type=MESH,
        )

    near = 2 * row // rows
    for turn in range(2):
        for sink in range(sinks):
            for way in range(2):
                there = row < rows - 1 if way == 0 else row > 0

                @pl.when(jnp.logical_and(there, (near + way + turn) % 2 == 1))
                def _():
                    hop(row, sink, way, snk_ref.at[sink]).start()

    def spread(step):
        return pltpu.make_async_remote_copy(
            src_ref=src_ref.at[0],
            dst_ref=src_all.at[col],
            send_sem=src_send.at[step],
            recv_sem=src_recv.at[col],
            device_id={"col": lax.rem(col + step, cols)},
            device_id_type=MESH,
        )

    for step in range(1, cols):
        spread(step).start()

    def arrive(step, sink):
        below, above = row - 1 - step, row + 1 + step

        @pl.when(below >= 0)
        def _():
            hop(below, sink, 0, snk_all.at[below, sink]).wait_recv()

            @pl.when(row < rows - 1)
            def _():
                hop(below, sink, 0, snk_all.at[below, sink]).start()

        @pl.when(above < rows)
        def _():
            hop(above, sink, 1, snk_all.at[above, sink]).wait_recv()

            @pl.when(row > 0)
            def _():
                hop(above, sink, 1, snk_all.at[above, sink]).start()

    for copy in locals_:
        copy.wait()

    lanes = lax.broadcasted_iota(jnp.int32, (1, order), 1)
    signs = jnp.where(lanes < 2 * evecs, 1.0, -1.0).astype(jnp.bfloat16)

    def sign_sink(sink, carry):
        for c in range(2):
            per_g[sink, c] = per[sink, c] * signs
        return carry

    lax.fori_loop(0, sinks, sign_sink, 0)

    codes = lax.broadcasted_iota(jnp.int32, (16, 16), 0)

    def chosen(which, table):
        onehot = jnp.where(codes == ins[which : which + 1, :], 1.0, 0.0).astype(jnp.bfloat16)
        return lax.dot_general(
            onehot, table[...].astype(jnp.bfloat16), (((0,), (0,)), ((), ())), preferred_element_type=jnp.float32
        )

    pick = chosen(1, second)
    for block in range(16):
        sel_second[block * 16 : (block + 1) * 16, :] = pick[
            :, block * 256 : (block + 1) * 256
        ].astype(jnp.bfloat16)
    sel_first[...] = chosen(0, first)

    def forward_sink(sink, carry):
        for shard in range(cols):
            u, first_group = divmod(shard * src_rows, evecs)
            first_group //= SUB
            pair = src_all[shard].reshape(2 * src_rows, order)
            with_re = jnp.dot(pair, per[sink, 0], preferred_element_type=jnp.float32)
            with_im = jnp.dot(pair, per[sink, 1], preferred_element_type=jnp.float32)
            both = (
                with_re[:src_rows] - with_im[src_rows:],
                with_im[:src_rows] + with_re[src_rows:],
            )
            for c in range(2):
                for h, piece in enumerate(split(both[c])):
                    for v in range(4):
                        for near in range(src_rows // SUB):
                            g = first_group + near
                            lhs[sink, u, v, c, h, :, g * evecs : (g + 1) * evecs] = piece[
                                near * SUB : (near + 1) * SUB, v * evecs : (v + 1) * evecs
                            ]
        return carry

    width = 16 * SUB
    same = lax.broadcasted_iota(jnp.int32, (SUB, width), 0) == lax.rem(
        lax.broadcasted_iota(jnp.int32, (SUB, width), 1), SUB
    )
    mask = jnp.where(same, 1.0, 0.0).astype(jnp.float32)

    at = lax.broadcasted_iota(jnp.int32, (width, 128), 0)
    to = lax.broadcasted_iota(jnp.int32, (width, 128), 1)
    fits = jnp.logical_and(at // 64 == lax.rem(to, 8) // 2, lax.rem(at // 32, 2) == lax.rem(to, 2))
    signed = jnp.where(fits, jnp.where(at < 128, 1.0, -1.0), 0.0).astype(jnp.float32)
    spins[...] = jnp.zeros_like(spins)

    def contract(sink, w, pair):
        with_re = dot_trans(per_g[sink, 0], pair)
        with_im = dot_trans(per_g[sink, 1], pair)
        both = (
            with_re[:, :evecs] + with_im[:, evecs:],
            with_re[:, evecs:] - with_im[:, :evecs],
        )
        for c in range(2):
            for h, piece in enumerate(split(both[c])):
                for s in range(4):
                    for g in range(groups):
                        start = s * evecs + g * SUB
                        rhs[s, c, h, :, g * evecs : (g + 1) * evecs] = piece[start : start + SUB]
        right = rhs[...].reshape(width, groups * evecs)
        sums = []
        left = lhs[sink].reshape(4 * width, groups * evecs)
        full = dot_trans(left, right).reshape(64, SUB, width)
        sums.append(jnp.sum(full * mask[None], axis=1))
        place = jnp.where(to // 8 == sink, signed, 0.0).astype(jnp.bfloat16)
        pair = jnp.concatenate(split(jnp.concatenate(sums, axis=0)), axis=1)
        spins[w] += jnp.dot(
            pair, jnp.concatenate([place, place], axis=0), preferred_element_type=jnp.float32
        )

    def whole_shard(shard, sink):
        contract(sink, shard, snk_all[shard, sink].reshape(2 * evecs, order))

    def both_ways(step, sink):
        def one(way, carry):
            shard = row + (2 * way - 1) * (1 + step)

            @pl.when(jnp.logical_and(shard >= 0, shard < rows))
            def _():
                whole_shard(shard, sink)

            return carry

        lax.fori_loop(0, 2, one, 0)

    def wait_sources():
        for step in range(1, cols):
            other = lax.rem(col + step, cols)
            pltpu.make_async_remote_copy(
                src_ref=src_ref.at[0],
                dst_ref=src_all.at[other],
                send_sem=src_send.at[step],
                recv_sem=src_recv.at[other],
                device_id={"col": other},
                device_id_type=MESH,
            ).wait_recv()

    if snk_rows == evecs:
        for sink in range(sinks):
            arrive(0, sink)
        wait_sources()
        lax.fori_loop(0, sinks, forward_sink, 0)

        def own(sink, carry):
            whole_shard(row, sink)
            return carry

        lax.fori_loop(0, sinks, own, 0)
        for step in range(1, rows - 2):
            for sink in range(sinks):
                arrive(step, sink)
                both_ways(step - 1, sink)
        for sink in range(sinks):
            if rows > 2:
                both_ways(rows - 3, sink)
        for sink in range(sinks):
            if rows > 2:
                arrive(rows - 2, sink)
            both_ways(rows - 2, sink)
    else:
        def pass_on(step, carry):
            for sink in range(sinks):
                arrive(step, sink)
            return carry

        lax.fori_loop(0, rows - 1, pass_on, 0)
        wait_sources()
        lax.fori_loop(0, sinks, forward_sink, 0)
        many = evecs // snk_rows

        def gathered(index, carry):
            sink, w = index // 4, lax.rem(index, 4)
            pieces = [snk_all[w * many + near, sink, c] for c in range(2) for near in range(many)]
            contract(sink, w, jnp.concatenate(pieces, axis=0))
            return carry

        lax.fori_loop(0, 4 * sinks, gathered, 0)

    halves = jnp.concatenate(split(spins[...].reshape(256, 128)), axis=1)
    mixed = jnp.dot(sel_second[...], halves, preferred_element_type=jnp.float32)
    mixed = mixed[:, :128] + mixed[:, 128:]
    totals = []
    for out in range(2):
        total = jnp.zeros((16, 128), jnp.float32)
        for block in range(16):
            start = (out * 16 + block) * 128
            total += sel_first[:, start : start + 128] * mixed[block * 16 : (block + 1) * 16]
        totals.append(total)
    sink_of = lax.broadcasted_iota(jnp.int32, (16, 128), 1) // 8
    member = jnp.where(sink_of == lax.broadcasted_iota(jnp.int32, (16, 128), 0), 1.0, 0.0)
    ends = dot_trans(
        member.astype(jnp.bfloat16), jnp.concatenate(split(jnp.concatenate(totals, axis=0)), axis=0)
    )
    ends = ends[:, :32] + ends[:, 32:]
    for out in range(2):
        out_ref[out] = ends[:sinks, out * 16 : (out + 1) * 16]

    for step in range(1, cols):
        spread(step).wait_send()

    def sent(shard, carry):
        for sink in range(sinks):

            @pl.when(jnp.logical_and(shard <= row, row < rows - 1))
            def _():
                hop(shard, sink, 0, snk_all.at[shard, sink]).wait_send()

            @pl.when(jnp.logical_and(shard >= row, row > 0))
            def _():
                hop(shard, sink, 1, snk_all.at[shard, sink]).wait_send()

        return carry

    lax.fori_loop(0, rows, sent, 0)


def shards(rows, cols, src_elem, snk_elem, peramb, insertions):
    sinks, order = peramb.shape[1], peramb.shape[-1]
    assert src_elem.shape[0] == 1 and sinks <= 16
    second, first = (jnp.asarray(table, jnp.float32) for table in insertion_tables(sinks))
    anywhere = pl.BlockSpec(memory_space=pltpu.HBM)
    vmem = pl.BlockSpec(memory_space=pltpu.VMEM)
    half = jnp.bfloat16
    wide = order * 2
    blocks = pl.pallas_call(
        functools.partial(kernel, rows, cols),
        out_shape=jax.ShapeDtypeStruct((2, sinks, 16), jnp.float32),
        in_specs=[anywhere] * 6,
        out_specs=vmem,
        scratch_shapes=[
            pltpu.VMEM((cols,) + src_elem.shape[1:], half),
            pltpu.VMEM((rows,) + snk_elem.shape, half),
            pltpu.VMEM(peramb.shape[1:], half),
            pltpu.VMEM(peramb.shape[1:], half),
            pltpu.VMEM((sinks, 4, 4, 2, 2, SUB, wide), half),
            pltpu.VMEM((4, 2, 2, SUB, wide), half),
            pltpu.VMEM((4, 64, 128), jnp.float32),
            pltpu.VMEM(insertions.shape, jnp.int32),
            pltpu.VMEM((16, 4096), jnp.float32),
            pltpu.VMEM((16, 4096), jnp.float32),
            pltpu.VMEM((256, 256), half),
            pltpu.VMEM((16, 4096), jnp.float32),
            pltpu.SemaphoreType.DMA((6,)),
            pltpu.SemaphoreType.DMA((cols,)),
            pltpu.SemaphoreType.DMA((cols,)),
            pltpu.SemaphoreType.DMA((2, rows, sinks)),
            pltpu.SemaphoreType.DMA((rows, sinks)),
        ],
        compiler_params=pltpu.CompilerParams(
            collective_id=0, has_side_effects=True, vmem_limit_bytes=64 * 1024 * 1024
        ),
    )(src_elem, snk_elem, peramb, insertions, second, first)
    return blocks.transpose(0, 2, 1)[:, :, None, :]


def solution(mesh):
    placed = (
        P("row", "grp", "col", None),
        P("col", "grp", "row", None),
        P("row", "col", "grp", None, None),
        P(),
    )
    body = functools.partial(shards, mesh.shape["row"], mesh.shape["col"])
    return jax.shard_map(
        body, mesh=mesh, in_specs=placed, out_specs=P(None, "grp", "row", "col"), check_vma=False
    )
```
